512 devices in a mesh: dp: 128 (over y, z_lo, x, core), tensor: 4 (over z_hi).
Axes of the slice: x: 4, y: 4, z: 16 (z_hi: 4, z_lo: 4; z = z_hi * 4 + z_lo), core: 2. Of those that a mesh axis runs over, the one named last changes fastest.
Arguments:
- queries: bfloat16 [16384, 2048], P('dp', 'tensor'), may hold values from -480 to 480
- encodings: bfloat16 [65536, 896], P('dp', 'tensor'), may hold values from -6 to 6
- kv_weight: bfloat16 [2, 896, 2048], P(None, None, 'tensor'), may hold values from -0.1875 to 0.1875
- w_out: bfloat16 [2048, 4096], P('tensor', 'dp'), may hold values from -0.5 to 0.5
- nbr_map: int32 [256, 16], P('dp'), may hold values from 0 to 4095, as said below
Outputs:
- attended: bfloat16 [16384, 4096], P('dp', 'tensor')
The draws below stay inside these ranges and needn't reach their ends.
Inputs may be any that keep to these rules, and one draw needn't show every extreme that they name: `nbr_map`: an entry is shard * 32 + row block within that shard. Among the 32 entries of the 2 spans on one index of dp, each shard is named exactly 1 times or not at all.
All inputs are finite; a program needn't handle non-finite values.
Results may differ from the reference program's by a relative error of at most 0.014.
The reference program's roundings to bfloat16 on the way count: a program that leaves them out, or rounds other values in their place, can miss the bound.
Values may be sent and summed in bfloat16 or wider, within the bound.
No kernel may reach another device: no remote copies, remote signals or barrier semaphores. Data moves between devices by JAX's collectives and lax.ppermute only.
A program may use at most 64 MiB of HBM per device.

```python
import math
import jax
import jax.numpy as jnp
from jax import lax

D = 4096
HEAD = 128
DE = 896
SPAN = 64
NLEN = 128
NEIGH = 2
HEADS = 16
ROWBLK = 16
CH_DEV = 2
HD = 2048
BPC = 16
REQ_DEV = 32
CAP = 1
EBLK = 32
TOKENS = 16384
NSPAN = 256
ENC_ROWS = 65536
N_DP = 128
N_TENSOR = 4


def draw_queries(key, part):
    key = jax.random.fold_in(key, 11)
    draw_key = jax.random.fold_in(key, 0)
    normal_part = jnp.clip(jax.random.normal(draw_key, (TOKENS, HD), jnp.float32), -6.0, 6.0)
    row_scale = 1.5
    return (normal_part * row_scale).astype(jnp.bfloat16)


def draw_nbr_map(key, part):
    key = jax.random.fold_in(key, 5)

    def one_device(device):
        dev_key = jax.random.fold_in(key, device)
        perm_key, order_key, block_key = jax.random.split(dev_key, 3)
        shard_perm = jax.random.permutation(perm_key, N_DP)
        request_order = jax.random.permutation(order_key, REQ_DEV)
        row_block = jax.random.randint(block_key, (REQ_DEV,), 0, EBLK)
        return shard_perm[request_order // CAP] * EBLK + row_block
    all_rows = jax.vmap(one_device)(jnp.arange(N_DP))
    return all_rows.reshape(NSPAN, BPC).astype(jnp.int32)


def levels(rng, extent, shards, low, largest):
    loudness, own = 1.0, jax.random.fold_in(rng, 6)
    for axis_at, shards_of in shards:
        draws = jnp.exp(jax.random.uniform(jax.random.fold_in(own, axis_at), (shards_of,), jnp.float32, low / len(shards), largest / len(shards)))
        loudness = loudness * jnp.repeat(draws, extent[axis_at] // shards_of).reshape([-1 if axis == axis_at else 1 for axis in range(len(extent))])
    return loudness


def noise(own_key, shape, width, bound, pieces=(), held_as=jnp.bfloat16):
    result = jax.random.normal(own_key, shape, jnp.float32) * width
    if len(pieces) > 0:
        result = levels(own_key, shape, pieces, -0.22, 0.18) * result
    return jnp.clip(result, min=-bound, max=bound).astype(held_as)


def setup_inputs(seed: int = 0) -> dict:
    keys = jax.random.split(jax.random.key(seed), 6)
    return {
        "queries": draw_queries(jax.random.fold_in(keys[5], 71), 0),
        "encodings": noise(keys[1], (ENC_ROWS, DE), 1.0, 6.0, ((0, 128), (1, 4))),
        "kv_weight": noise(keys[2], (2, DE, HD), DE ** -0.5, 0.1875, ((2, 4),)),
        "w_out": noise(keys[3], (HD, D), HEAD ** -0.5, 0.5, ((0, 4), (1, 128))),
        "nbr_map": draw_nbr_map(jax.random.fold_in(keys[5], 71), 0),
    }


def reference(queries, encodings, kv_weight, w_out, nbr_map):
    row_blocks = encodings.reshape(N_DP * EBLK, ROWBLK, DE)
    q_groups = queries.reshape(N_DP, CH_DEV, SPAN, HEADS, HEAD)
    map_groups = nbr_map.reshape(N_DP, CH_DEV * BPC)
    split_out = w_out.astype(jnp.float32).reshape(N_TENSOR, HD // N_TENSOR, D)
    inv_scale = 1.0 / math.sqrt(HEAD)

    def one_group(group_pair):
        q_dev, picked = group_pair
        neighbours = row_blocks[picked].reshape(CH_DEV * NEIGH * NLEN, DE)
        key_rows = jnp.dot(neighbours, kv_weight[0], preferred_element_type=jnp.float32).astype(jnp.bfloat16)
        value_rows = jnp.dot(neighbours, kv_weight[1], preferred_element_type=jnp.float32).astype(jnp.bfloat16)
        key_rows = key_rows.reshape(CH_DEV, NEIGH * NLEN, HEADS, HEAD)
        value_rows = value_rows.reshape(CH_DEV, NEIGH * NLEN, HEADS, HEAD)
        scores = jnp.einsum('cqhd,ckhd->chqk', q_dev.astype(jnp.float32), key_rows.astype(jnp.float32)) * inv_scale
        row_max = lax.optimization_barrier(jnp.max(scores, axis=-1, keepdims=True))
        exponent = jnp.exp(scores - row_max)
        weights = (exponent / lax.optimization_barrier(jnp.sum(exponent, axis=-1, keepdims=True))).astype(jnp.bfloat16)
        attn_mix = jnp.einsum('chqk,ckhd->cqhd', weights.astype(jnp.float32), value_rows.astype(jnp.float32)).astype(jnp.bfloat16)
        attn_mix = attn_mix.reshape(CH_DEV * SPAN, N_TENSOR, HD // N_TENSOR)
        partial_value = jnp.einsum('tgk,gkd->gtd', attn_mix.astype(jnp.float32), split_out).astype(jnp.bfloat16)
        partial_value = lax.optimization_barrier(partial_value)
        return lax.optimization_barrier(jnp.sum(partial_value.astype(jnp.float32), axis=0)).astype(jnp.bfloat16)
    attended = lax.map(one_group, (q_groups, map_groups))
    return attended.reshape(TOKENS, D)
```

```python
import functools
import math

import jax
import jax.numpy as jnp
from jax import lax
from jax.experimental import pallas as pl
from jax.experimental.pallas import tpu as pltpu
from jax.sharding import Mesh
from jax.sharding import PartitionSpec as P

HEAD = 128
SPAN = 64
ROWBLK = 16
NY, NZ, NX, NC, NT = 4, 4, 4, 2, 4
DP = ("y", "z", "x", "c")
LAST_DIMS = (((1,), (1,)), ((), ()))


def attend_kernel(q_ref, feat_ref, kv_ref, mixed_ref):
    spans = q_ref.shape[0] // SPAN
    per_span = feat_ref.shape[1] // spans
    heads = q_ref.shape[1] // HEAD
    feats = feat_ref[...].T
    keys = jnp.dot(feats, kv_ref[0], preferred_element_type=jnp.float32)
    keys = keys.astype(jnp.bfloat16)
    values = jnp.dot(feats, kv_ref[1], preferred_element_type=jnp.float32)
    values = values.astype(jnp.bfloat16)
    for span in range(spans):
        for head in range(heads):
            tokens = slice(span * SPAN, (span + 1) * SPAN)
            rows = slice(span * per_span, (span + 1) * per_span)
            lanes = slice(head * HEAD, (head + 1) * HEAD)
            scores = lax.dot_general(
                q_ref[tokens, lanes], keys[rows, lanes], LAST_DIMS,
                preferred_element_type=jnp.float32,
            ) * (1.0 / math.sqrt(HEAD))
            exponent = jnp.exp(scores - jnp.max(scores, axis=-1, keepdims=True))
            weights = exponent / jnp.sum(exponent, axis=-1, keepdims=True)
            mixed = jnp.dot(
                weights.astype(jnp.bfloat16), values[rows, lanes],
                preferred_element_type=jnp.float32,
            )
            mixed_ref[tokens, lanes] = mixed.astype(jnp.bfloat16)


def attend(queries, feats, kv_weight):
    return pl.pallas_call(
        attend_kernel,
        out_shape=jax.ShapeDtypeStruct(queries.shape, jnp.bfloat16),
        compiler_params=pltpu.CompilerParams(vmem_limit_bytes=32 * 2**20),
        name="attend",
    )(queries, feats, kv_weight)


def project_kernel(mixed_ref, w_ref, out_ref):
    total = None
    for group in range(mixed_ref.shape[0]):
        partial = lax.dot_general(
            mixed_ref[group], w_ref[0, group], LAST_DIMS,
            preferred_element_type=jnp.float32,
        )
        partial = partial.astype(jnp.bfloat16).astype(jnp.float32)
        total = partial if total is None else total + partial
    out_ref[...] = total.astype(jnp.bfloat16)


def project(mixed, w_cols):
    groups, tokens, width = mixed.shape
    blocks, _, cols, _ = w_cols.shape
    return pl.pallas_call(
        project_kernel,
        grid=(blocks,),
        in_specs=[
            pl.BlockSpec((groups, tokens, width), lambda i: (0, 0, 0)),
            pl.BlockSpec((1, groups, cols, width), lambda i: (i, 0, 0, 0)),
        ],
        out_specs=pl.BlockSpec((tokens, cols), lambda i: (0, i)),
        out_shape=jax.ShapeDtypeStruct((tokens, blocks * cols), jnp.bfloat16),
        compiler_params=pltpu.CompilerParams(vmem_limit_bytes=32 * 2**20),
        name="project",
    )(mixed, w_cols)


def device_index(y, z, x, c, t):
    return (((y * NZ + z) * NX + x) * NC + c) * NT + t


def to_column_owner():
    pairs = []
    for y in range(NY):
        for block in range(NZ * NX * NC):
            z, x, c = block // (NX * NC), block // NC % NX, block % NC
            xc, new_z = block // NZ, block % NZ
            for t in range(NT):
                target = device_index(t, new_z, xc // NC, xc % NC, y)
                pairs.append((device_index(y, z, x, c, t), target))
    return pairs


def shards(queries, encodings, kv_weight, w_out, nbr_map):
    dp_count = lax.axis_size(DP)
    enc_blocks = encodings.shape[0] // ROWBLK
    features = encodings.shape[1]
    flat_map = nbr_map.reshape(-1)
    source_shard = flat_map // enc_blocks
    row_block = flat_map % enc_blocks

    shard_ids = jnp.arange(dp_count, dtype=jnp.int32)
    wanted = jnp.sum(
        jnp.where(source_shard[:, None] == shard_ids[None, :], row_block[:, None], 0), axis=0
    )
    served = lax.all_to_all(
        wanted.reshape(dp_count, 1), DP, split_axis=0, concat_axis=0, tiled=True
    ).reshape(dp_count)

    piece = lax.ppermute(w_out.T, DP + ("t",), to_column_owner())
    piece = lax.all_gather(piece, "z", axis=0, tiled=True)
    w_cols = lax.all_gather(piece, ("x", "c", "y"), axis=0, tiled=True)
    w_cols = w_cols.reshape(NX * NC, NY, piece.shape[0], piece.shape[1])

    chosen = encodings.reshape(enc_blocks, ROWBLK, features)[served]
    arrived = lax.all_to_all(chosen, DP, split_axis=0, concat_axis=0, tiled=True)
    gathered = arrived[source_shard].reshape(-1, features).T
    feats = lax.all_gather(gathered, "t", axis=0, tiled=True)

    mixed = attend(queries, feats, kv_weight)
    mixed = lax.all_gather(mixed, "t", axis=0, tiled=False)
    return project(mixed, w_cols)


def solution(mesh):
    fine = Mesh(mesh.devices.reshape(NY, NZ, NX, NC, NT), DP + ("t",))
    return jax.shard_map(
        shards,
        mesh=fine,
        in_specs=(
            P(DP, "t"),
            P(DP, "t"),
            P(None, None, "t"),
            P("t", DP),
            P(DP, None),
        ),
        out_specs=P(DP, "t"),
        check_vma=False,
    )
```

```python
import functools
import math

import jax
import jax.numpy as jnp
from jax import lax
from jax.experimental import pallas as pl
from jax.experimental.pallas import tpu as pltpu
from jax.sharding import Mesh
from jax.sharding import PartitionSpec as P

HEAD = 128
SPAN = 64
ROWBLK = 16
NY, NZ, NX, NC, NT = 4, 4, 4, 2, 4
DP = ("y", "z", "x", "c")
PEERS = ("y", "x", "c")
LAST_DIMS = (((1,), (1,)), ((), ()))


def attend_kernel(q_ref, feat_ref, kv_ref, mixed_ref):
    spans = q_ref.shape[0] // SPAN
    per_span = feat_ref.shape[1] // spans
    heads = q_ref.shape[1] // HEAD
    feats = feat_ref[...].T
    keys = jnp.dot(feats, kv_ref[0], preferred_element_type=jnp.float32)
    keys = keys.astype(jnp.bfloat16)
    values = jnp.dot(feats, kv_ref[1], preferred_element_type=jnp.float32)
    values = values.astype(jnp.bfloat16)
    for span in range(spans):
        for head in range(heads):
            tokens = slice(span * SPAN, (span + 1) * SPAN)
            rows = slice(span * per_span, (span + 1) * per_span)
            lanes = slice(head * HEAD, (head + 1) * HEAD)
            scores = lax.dot_general(
                q_ref[tokens, lanes], keys[rows, lanes], LAST_DIMS,
                preferred_element_type=jnp.float32,
            ) * (1.0 / math.sqrt(HEAD))
            exponent = jnp.exp(scores - jnp.max(scores, axis=-1, keepdims=True))
            weights = exponent / jnp.sum(exponent, axis=-1, keepdims=True)
            mixed = jnp.dot(
                weights.astype(jnp.bfloat16), values[rows, lanes],
                preferred_element_type=jnp.float32,
            )
            mixed_ref[tokens, lanes] = mixed.astype(jnp.bfloat16)


def attend(queries, feats, kv_weight):
    return pl.pallas_call(
        attend_kernel,
        out_shape=jax.ShapeDtypeStruct(queries.shape, jnp.bfloat16),
        compiler_params=pltpu.CompilerParams(vmem_limit_bytes=32 * 2**20),
        name="attend",
    )(queries, feats, kv_weight)


def pick_kernel(served_ref, feats_ref, piece_ref, chosen_ref, piece_out_ref, rows_ref):
    shards_here, _, rows = feats_ref.shape
    for z in range(shards_here):
        rows_ref[z * rows : (z + 1) * rows] = feats_ref[z].T
    for peer in range(chosen_ref.shape[0]):
        for z in range(shards_here):
            start = pl.multiple_of(served_ref[peer, 0, z] * ROWBLK, ROWBLK)
            chosen_ref[peer, z] = rows_ref[pl.ds(z * rows + start, ROWBLK)]
    piece_out_ref[...] = piece_ref[...]


def pick(served, feats, piece):
    shards_here, features, rows = feats.shape
    return pl.pallas_call(
        pick_kernel,
        in_specs=[
            pl.BlockSpec(memory_space=pltpu.SMEM),
            pl.BlockSpec(memory_space=pltpu.VMEM),
            pl.BlockSpec(memory_space=pltpu.VMEM),
        ],
        out_shape=(
            jax.ShapeDtypeStruct(
                (served.shape[0], shards_here, ROWBLK, features), feats.dtype
            ),
            jax.ShapeDtypeStruct(piece.shape, piece.dtype),
        ),
        scratch_shapes=[pltpu.VMEM((shards_here * rows, features), feats.dtype)],
        compiler_params=pltpu.CompilerParams(vmem_limit_bytes=32 * 2**20),
        name="pick",
    )(served, feats, piece)


def take_kernel(slot_ref, arrived_ref, four_ref, feats_ref, four_out_ref, rows_ref):
    for at in range(slot_ref.shape[0]):
        rows_ref[at * ROWBLK : (at + 1) * ROWBLK] = arrived_ref[slot_ref[at]]
    feats_ref[...] = rows_ref[...].T
    four_out_ref[...] = four_ref[...]


def take(slots, arrived, four):
    rows, features = slots.shape[0] * ROWBLK, arrived.shape[2]
    return pl.pallas_call(
        take_kernel,
        in_specs=[
            pl.BlockSpec(memory_space=pltpu.SMEM),
            pl.BlockSpec(memory_space=pltpu.VMEM),
            pl.BlockSpec(memory_space=pltpu.VMEM),
        ],
        out_shape=(
            jax.ShapeDtypeStruct((features, rows), arrived.dtype),
            jax.ShapeDtypeStruct(four.shape, four.dtype),
        ),
        scratch_shapes=[pltpu.VMEM((rows, features), arrived.dtype)],
        compiler_params=pltpu.CompilerParams(vmem_limit_bytes=32 * 2**20),
        name="take",
    )(slots, arrived, four)


def project_kernel(mixed_ref, w_ref, out_ref):
    places, groups, _, cols, width = w_ref.shape
    total = None
    for group in range(groups):
        partial = lax.dot_general(
            mixed_ref[group], w_ref[:, group, 0].reshape(places * cols, width),
            LAST_DIMS, preferred_element_type=jnp.float32,
        )
        partial = partial.astype(jnp.bfloat16).astype(jnp.float32)
        total = partial if total is None else total + partial
    out_ref[...] = total.astype(jnp.bfloat16)


def project(mixed, w_cols):
    groups, tokens, width = mixed.shape
    places, _, blocks, cols, _ = w_cols.shape
    return pl.pallas_call(
        project_kernel,
        grid=(blocks,),
        in_specs=[
            pl.BlockSpec((groups, tokens, width), lambda i: (0, 0, 0)),
            pl.BlockSpec((places, groups, 1, cols, width), lambda i: (0, 0, i, 0, 0)),
        ],
        out_specs=pl.BlockSpec((tokens, places * cols), lambda i: (0, i)),
        out_shape=jax.ShapeDtypeStruct((tokens, places * blocks * cols), jnp.bfloat16),
        compiler_params=pltpu.CompilerParams(vmem_limit_bytes=60 * 2**20),
        name="project",
    )(mixed, w_cols)


def device_index(y, z, x, c, t):
    return (((y * NZ + z) * NX + x) * NC + c) * NT + t


def to_column_owner():
    return [
        (device_index(y, z, x, c, t), device_index(t, z, x, c, y))
        for y in range(NY) for z in range(NZ) for x in range(NX) for c in range(NC)
        for t in range(NT)
    ]


def shards(queries, encodings, kv_weight, w_out, nbr_map):
    enc_blocks = encodings.shape[0] // ROWBLK
    flat_map = nbr_map.reshape(-1)
    shard = flat_map // enc_blocks
    row_block = flat_map % enc_blocks
    peer = shard // (NZ * NX * NC) * (NX * NC) + shard % (NX * NC)
    slots = peer * NZ + shard // (NX * NC) % NZ

    lanes = jnp.arange(NY * NX * NC * 128, dtype=jnp.int32)
    lane_slot = jnp.where(lanes % 128 < NZ, lanes // 128 * NZ + lanes % 128, -1)
    wanted = jnp.sum(
        jnp.where(slots[:, None] == lane_slot[None, :], row_block[:, None], 0), axis=0
    )
    served = lax.all_to_all(
        wanted.reshape(NY * NX * NC, 1, 128), PEERS, split_axis=0, concat_axis=0, tiled=True
    )
    enc_z = lax.all_gather(encodings.T, "z", axis=0, tiled=False)

    piece = lax.ppermute(w_out.T, DP + ("t",), to_column_owner())

    chosen, piece = pick(served, enc_z, piece)
    arrived = lax.all_to_all(chosen, PEERS, split_axis=0, concat_axis=0, tiled=True)
    arrived = arrived.reshape(-1, ROWBLK, encodings.shape[1])
    four = lax.all_gather(piece, "z", axis=0, tiled=True)

    gathered, four = take(slots, arrived, four)
    w_cols = lax.all_gather(four, ("x", "c", "y"), axis=0, tiled=True)
    w_cols = w_cols.reshape(NX * NC, NY, NZ, w_out.shape[1], w_out.shape[0])
    feats = lax.all_gather(gathered, "t", axis=0, tiled=True)

    mixed = attend(queries, feats, kv_weight)
    mixed = lax.all_gather(mixed, "t", axis=0, tiled=False)
    return project(mixed, w_cols)


def solution(mesh):
    fine = Mesh(mesh.devices.reshape(NY, NZ, NX, NC, NT), DP + ("t",))
    return jax.shard_map(
        shards,
        mesh=fine,
        in_specs=(
            P(DP, "t"),
            P(DP, "t"),
            P(None, None, "t"),
            P("t", DP),
            P(DP, None),
        ),
        out_specs=P(DP, "t"),
        check_vma=False,
    )
```

```python
import functools
import math

import jax
import jax.numpy as jnp
from jax import lax
from jax.experimental import pallas as pl
from jax.experimental.pallas import tpu as pltpu
from jax.sharding import Mesh
from jax.sharding import PartitionSpec as P

HEAD = 128
SPAN = 64
ROWBLK = 16
NY, NZ, NX, NC, NT = 4, 4, 4, 2, 4
DP = ("y", "z", "x", "c")
PEERS = ("y", "x", "c")
LAST_DIMS = (((1,), (1,)), ((), ()))


def attend_kernel(q_ref, feat_ref, kv_ref, cols_ref, mixed_ref, cols_out_ref):
    del cols_ref, cols_out_ref
    spans = q_ref.shape[0] // SPAN
    per_span = feat_ref.shape[1] // spans
    heads = q_ref.shape[1] // HEAD
    feats = feat_ref[...].T
    keys = jnp.dot(feats, kv_ref[0], preferred_element_type=jnp.float32)
    keys = keys.astype(jnp.bfloat16)
    values = jnp.dot(feats, kv_ref[1], preferred_element_type=jnp.float32)
    values = values.astype(jnp.bfloat16)
    for span in range(spans):
        for head in range(heads):
            tokens = slice(span * SPAN, (span + 1) * SPAN)
            rows = slice(span * per_span, (span + 1) * per_span)
            lanes = slice(head * HEAD, (head + 1) * HEAD)
            scores = lax.dot_general(
                q_ref[tokens, lanes], keys[rows, lanes], LAST_DIMS,
                preferred_element_type=jnp.float32,
            ) * (1.0 / math.sqrt(HEAD))
            exponent = jnp.exp(scores - jnp.max(scores, axis=-1, keepdims=True))
            weights = exponent / jnp.sum(exponent, axis=-1, keepdims=True)
            mixed = jnp.dot(
                weights.astype(jnp.bfloat16), values[rows, lanes],
                preferred_element_type=jnp.float32,
            )
            mixed_ref[tokens, lanes] = mixed.astype(jnp.bfloat16)


def attend(queries, feats, kv_weight, cols):
    in_vmem, anywhere = pl.BlockSpec(memory_space=pltpu.VMEM), pl.BlockSpec(memory_space=pl.ANY)
    return pl.pallas_call(
        attend_kernel,
        in_specs=[in_vmem, in_vmem, in_vmem, anywhere],
        out_specs=(in_vmem, anywhere),
        out_shape=(
            jax.ShapeDtypeStruct(queries.shape, jnp.bfloat16),
            jax.ShapeDtypeStruct(cols.shape, cols.dtype),
        ),
        input_output_aliases={3: 1},
        compiler_params=pltpu.CompilerParams(vmem_limit_bytes=32 * 2**20),
        name="attend",
    )(queries, feats, kv_weight, cols)


def pick_kernel(served_ref, feats_ref, piece_ref, chosen_ref, piece_out_ref, rows_ref):
    shards_here, _, rows = feats_ref.shape
    for z in range(shards_here):
        rows_ref[z * rows : (z + 1) * rows] = feats_ref[z].T
    for peer in range(chosen_ref.shape[0]):
        for z in range(shards_here):
            start = pl.multiple_of(served_ref[peer, 0, z] * ROWBLK, ROWBLK)
            chosen_ref[peer, z] = rows_ref[pl.ds(z * rows + start, ROWBLK)]
    piece_out_ref[...] = piece_ref[...]


def pick(served, feats, piece):
    shards_here, features, rows = feats.shape
    return pl.pallas_call(
        pick_kernel,
        in_specs=[
            pl.BlockSpec(memory_space=pltpu.SMEM),
            pl.BlockSpec(memory_space=pltpu.VMEM),
            pl.BlockSpec(memory_space=pltpu.VMEM),
        ],
        out_shape=(
            jax.ShapeDtypeStruct(
                (served.shape[0], shards_here, ROWBLK, features), feats.dtype
            ),
            jax.ShapeDtypeStruct(piece.shape, piece.dtype),
        ),
        scratch_shapes=[pltpu.VMEM((shards_here * rows, features), feats.dtype)],
        compiler_params=pltpu.CompilerParams(vmem_limit_bytes=32 * 2**20),
        name="pick",
    )(served, feats, piece)


def take_kernel(slot_ref, arrived_ref, pieces_ref, feats_ref, pieces_out_ref, rows_ref):
    del pieces_ref, pieces_out_ref
    for at in range(slot_ref.shape[0]):
        rows_ref[at * ROWBLK : (at + 1) * ROWBLK] = arrived_ref[slot_ref[at]]
    feats_ref[...] = rows_ref[...].T


def take(slots, arrived, pieces):
    rows, features = slots.shape[0] * ROWBLK, arrived.shape[2]
    return pl.pallas_call(
        take_kernel,
        in_specs=[
            pl.BlockSpec(memory_space=pltpu.SMEM),
            pl.BlockSpec(memory_space=pltpu.VMEM),
            pl.BlockSpec(memory_space=pl.ANY),
        ],
        out_specs=(
            pl.BlockSpec(memory_space=pltpu.VMEM),
            pl.BlockSpec(memory_space=pl.ANY),
        ),
        out_shape=(
            jax.ShapeDtypeStruct((features, rows), arrived.dtype),
            jax.ShapeDtypeStruct(pieces.shape, pieces.dtype),
        ),
        input_output_aliases={2: 1},
        scratch_shapes=[pltpu.VMEM((rows, features), arrived.dtype)],
        compiler_params=pltpu.CompilerParams(vmem_limit_bytes=32 * 2**20),
        name="take",
    )(slots, arrived, pieces)


def project_kernel(core_ref, mixed_ref, own_ref, other_ref, out_ref):
    groups, cols, _ = own_ref.shape
    step = 256
    for half, w_ref in ((core_ref[0], own_ref), (1 - core_ref[0], other_ref)):
        for col in range(0, cols, step):
            total = None
            for group in range(groups):
                partial = lax.dot_general(
                    mixed_ref[group], w_ref[group, col : col + step], LAST_DIMS,
                    preferred_element_type=jnp.float32,
                )
                partial = partial.astype(jnp.bfloat16).astype(jnp.float32)
                total = partial if total is None else total + partial
            start = pl.multiple_of(half * cols + col, step)
            out_ref[:, pl.ds(start, step)] = total.astype(jnp.bfloat16)


def project(core, mixed, own, other):
    return pl.pallas_call(
        project_kernel,
        in_specs=[pl.BlockSpec(memory_space=pltpu.SMEM)]
        + [pl.BlockSpec(memory_space=pltpu.VMEM)] * 3,
        out_shape=jax.ShapeDtypeStruct((mixed.shape[1], NC * own.shape[1]), jnp.bfloat16),
        compiler_params=pltpu.CompilerParams(vmem_limit_bytes=32 * 2**20),
        name="project",
    )(core, mixed, own, other)


def device_index(y, z, x, c, t):
    return (((y * NZ + z) * NX + x) * NC + c) * NT + t


def to_column_owner():
    pairs = []
    for y in range(NY):
        for block in range(NZ * NX * NC):
            z, x, c = block // (NX * NC), block // NC % NX, block % NC
            new_c, new_x, new_z = block // (NX * NZ), block // NZ % NX, block % NZ
            for t in range(NT):
                target = device_index(t, new_z, new_x, new_c, y)
                pairs.append((device_index(y, z, x, c, t), target))
    return pairs


def shards(queries, encodings, kv_weight, w_out, nbr_map):
    enc_blocks = encodings.shape[0] // ROWBLK
    flat_map = nbr_map.reshape(-1)
    shard = flat_map // enc_blocks
    row_block = flat_map % enc_blocks
    peer = shard // (NZ * NX * NC) * (NX * NC) + shard % (NX * NC)
    slots = peer * NZ + shard // (NX * NC) % NZ

    lanes = jnp.arange(NY * NX * NC * 128, dtype=jnp.int32)
    lane_slot = jnp.where(lanes % 128 < NZ, lanes // 128 * NZ + lanes % 128, -1)
    wanted = jnp.sum(
        jnp.where(slots[:, None] == lane_slot[None, :], row_block[:, None], 0), axis=0
    )
    served = lax.all_to_all(
        wanted.reshape(NY * NX * NC, 1, 128), PEERS, split_axis=0, concat_axis=0, tiled=True
    )
    enc_z = lax.all_gather(encodings.T, "z", axis=0, tiled=False)

    piece = lax.ppermute(w_out.T, DP + ("t",), to_column_owner())

    chosen, piece = pick(served, enc_z, piece)
    arrived = lax.all_to_all(chosen, PEERS, split_axis=0, concat_axis=0, tiled=True)
    arrived = arrived.reshape(-1, ROWBLK, encodings.shape[1])
    four = lax.all_gather(piece, "z", axis=0, tiled=True)
    four = jnp.broadcast_to(four[None], (NY * NX,) + four.shape)

    gathered, four = take(slots, arrived, four)
    own = lax.all_to_all(four, ("y", "x"), split_axis=0, concat_axis=0, tiled=True)
    own = own.reshape(NY, -1, own.shape[2])
    feats = lax.all_gather(gathered, "t", axis=0, tiled=True)

    mixed, own = attend(queries, feats, kv_weight, own)
    other = lax.ppermute(own, "c", [(0, 1), (1, 0)])
    mixed = lax.all_gather(mixed, "t", axis=0, tiled=False)
    core = lax.axis_index("c").astype(jnp.int32).reshape(1)
    return project(core, mixed, own, other)


def solution(mesh):
    fine = Mesh(mesh.devices.reshape(NY, NZ, NX, NC, NT), DP + ("t",))
    return jax.shard_map(
        shards,
        mesh=fine,
        in_specs=(
            P(DP, "t"),
            P(DP, "t"),
            P(None, None, "t"),
            P("t", DP),
            P(DP, None),
        ),
        out_specs=P(DP, "t"),
        check_vma=False,
    )
```

```python
import math

import jax
import jax.numpy as jnp
from jax import lax
from jax.experimental import pallas as pl
from jax.experimental.pallas import tpu as pltpu
from jax.sharding import Mesh
from jax.sharding import PartitionSpec as P

HEAD = 128
SPAN = 64
ROWBLK = 16
LANES = 128
W_PARTS = 2
NY, NZ, NX, NC, NT = 4, 4, 4, 2, 4
DP = ("y", "z", "x", "c")
PEERS = ("y", "x", "c")
LAST_DIMS = (((1,), (1,)), ((), ()))
IN_SMEM = pl.BlockSpec(memory_space=pltpu.SMEM)
IN_VMEM = pl.BlockSpec(memory_space=pltpu.VMEM)
IN_HBM = pl.BlockSpec(memory_space=pltpu.HBM)
ANYWHERE = pl.BlockSpec(memory_space=pl.ANY)
PARAMS = pltpu.CompilerParams(vmem_limit_bytes=24 * 2**20)


def like(value):
    return jax.ShapeDtypeStruct(value.shape, value.dtype)


def slot_of(shard):
    per_y = NZ * NX * NC
    peer = shard // per_y * (NX * NC) + shard % (NX * NC)
    return peer * NZ + shard // (NX * NC) % NZ


def want(nbr_map, enc_blocks):
    blocks = nbr_map.astype(jnp.uint32)
    lane = jnp.arange(LANES, dtype=jnp.uint32)[None, :]
    code = jnp.arange(NY * NX * NC, dtype=jnp.uint32)[:, None] * NZ + lane
    code = jnp.where(lane < NZ, code, NY * NX * NC * NZ)
    here = slot_of(blocks // enc_blocks)[:, :, None, None] == code
    wanted = jnp.where(here, (blocks % enc_blocks)[:, :, None, None], 0)
    return jnp.sum(wanted, axis=(0, 1)).astype(jnp.int32)[:, None, :]


def attend_kernel(q_ref, feat_ref, kv_ref, mixed_ref):
    spans = q_ref.shape[0] // SPAN
    per_span = feat_ref.shape[1] // spans
    heads = q_ref.shape[1] // HEAD
    feats = feat_ref[...].T
    keys = jnp.dot(feats, kv_ref[0], preferred_element_type=jnp.float32)
    keys = keys.astype(jnp.bfloat16)
    values = jnp.dot(feats, kv_ref[1], preferred_element_type=jnp.float32)
    values = values.astype(jnp.bfloat16)
    for span in range(spans):
        for head in range(heads):
            tokens = slice(span * SPAN, (span + 1) * SPAN)
            rows = slice(span * per_span, (span + 1) * per_span)
            lanes = slice(head * HEAD, (head + 1) * HEAD)
            scores = lax.dot_general(
                q_ref[tokens, lanes], keys[rows, lanes], LAST_DIMS,
                preferred_element_type=jnp.float32,
            ) * (1.0 / math.sqrt(HEAD))
            exponent = jnp.exp(scores - jnp.max(scores, axis=-1, keepdims=True))
            weights = exponent / jnp.sum(exponent, axis=-1, keepdims=True)
            mixed = jnp.dot(
                weights.astype(jnp.bfloat16), values[rows, lanes],
                preferred_element_type=jnp.float32,
            )
            mixed_ref[tokens, lanes] = mixed.astype(jnp.bfloat16)


def attend(queries, feats, kv_weight):
    return pl.pallas_call(
        attend_kernel,
        in_specs=[IN_VMEM, IN_VMEM, IN_VMEM],
        out_shape=like(queries),
        compiler_params=PARAMS,
        name="attend",
    )(queries, feats, kv_weight)


def pick_kernel(served_ref, feats_ref, piece_ref, chosen_ref, piece_out_ref, rows_ref):
    shards_here, _, rows = feats_ref.shape
    for z in range(shards_here):
        rows_ref[z * rows : (z + 1) * rows] = feats_ref[z].T
    for peer in range(chosen_ref.shape[0]):
        for z in range(shards_here):
            start = pl.multiple_of(served_ref[peer, 0, z] * ROWBLK, ROWBLK)
            chosen_ref[peer, z] = rows_ref[pl.ds(z * rows + start, ROWBLK)]
    piece_out_ref[...] = piece_ref[...]


def pick(served, feats, piece):
    shards_here, features, rows = feats.shape
    chosen = (served.shape[0], shards_here, ROWBLK, features)
    return pl.pallas_call(
        pick_kernel,
        in_specs=[IN_SMEM, IN_VMEM, IN_VMEM],
        out_shape=(jax.ShapeDtypeStruct(chosen, feats.dtype), like(piece)),
        scratch_shapes=[pltpu.VMEM((shards_here * rows, features), feats.dtype)],
        compiler_params=PARAMS,
        name="pick",
    )(served, feats, piece)


def take_kernel(slot_ref, arrived_ref, feats_ref, rows_ref):
    spans, per_span = slot_ref.shape
    for span in range(spans):
        for at in range(per_span):
            to = (span * per_span + at) * ROWBLK
            rows_ref[to : to + ROWBLK] = arrived_ref[slot_ref[span, at]]
    feats_ref[...] = rows_ref[...].T


def take(slots, arrived):
    rows, features = slots.size * ROWBLK, arrived.shape[2]
    return pl.pallas_call(
        take_kernel,
        in_specs=[IN_SMEM, IN_VMEM],
        out_shape=jax.ShapeDtypeStruct((features, rows), arrived.dtype),
        scratch_shapes=[pltpu.VMEM((rows, features), arrived.dtype)],
        compiler_params=PARAMS,
        name="take",
    )(slots, arrived)


def project_kernel(mixed_ref, far_ref, out_ref, w_ref, sems):
    parts, groups, cols, _ = w_ref.shape
    copies = [
        pltpu.make_async_copy(
            far_ref.at[:, pl.ds(part * cols, cols)], w_ref.at[part], sems.at[part]
        )
        for part in range(parts)
    ]
    for copy in copies:
        copy.start()
    step = 256
    for part in range(parts):
        copies[part].wait()
        for col in range(0, cols, step):
            total = None
            for group in range(groups):
                partial = lax.dot_general(
                    mixed_ref[group], w_ref[part, group, col : col + step], LAST_DIMS,
                    preferred_element_type=jnp.float32,
                )
                partial = partial.astype(jnp.bfloat16).astype(jnp.float32)
                total = partial if total is None else total + partial
            to = part * cols + col
            out_ref[:, to : to + step] = total.astype(jnp.bfloat16)


def project(mixed, w_cols):
    groups, cols, width = w_cols.shape
    return pl.pallas_call(
        project_kernel,
        in_specs=[IN_VMEM, IN_HBM],
        out_shape=jax.ShapeDtypeStruct((mixed.shape[1], cols), jnp.bfloat16),
        scratch_shapes=[
            pltpu.VMEM((W_PARTS, groups, cols // W_PARTS, width), w_cols.dtype),
            pltpu.SemaphoreType.DMA((W_PARTS,)),
        ],
        compiler_params=PARAMS,
        name="project",
    )(mixed, pltpu.with_memory_space_constraint(w_cols, pltpu.HBM))


def device_index(y, z, x, c, t):
    return (((y * NZ + z) * NX + x) * NC + c) * NT + t


def to_column_owner():
    pairs = []
    for y in range(NY):
        for block in range(NZ * NX * NC):
            z, x, c = block // (NX * NC), block // NC % NX, block % NC
            new_x, new_c, new_z = block // (NC * NZ), block // NZ % NC, block % NZ
            for t in range(NT):
                target = device_index(t, new_z, new_x, new_c, y)
                pairs.append((device_index(y, z, x, c, t), target))
    return pairs


def shards(queries, encodings, kv_weight, w_out, nbr_map):
    enc_blocks = encodings.shape[0] // ROWBLK
    enc_z = lax.all_gather(encodings.T, "z", axis=0, tiled=False)
    served = lax.all_to_all(
        want(nbr_map, enc_blocks), PEERS, split_axis=0, concat_axis=0, tiled=True
    )

    piece = lax.ppermute(w_out.T, DP + ("t",), to_column_owner())

    chosen, piece = pick(served, enc_z, piece)
    arrived = lax.all_to_all(chosen, PEERS, split_axis=0, concat_axis=0, tiled=True)
    four = lax.all_gather(piece, "z", axis=0, tiled=True)
    pieces = jnp.broadcast_to(four[None], (NY * NX * NC,) + four.shape)

    slots = slot_of(nbr_map // enc_blocks)
    slots, pieces = lax.optimization_barrier((slots, pieces))
    gathered = take(slots, arrived.reshape(-1, ROWBLK, encodings.shape[1]))
    gathered, pieces = lax.optimization_barrier((gathered, pieces))
    w_cols = lax.all_to_all(pieces, PEERS, split_axis=0, concat_axis=0, tiled=True)
    w_cols = w_cols.reshape(NY, -1, w_cols.shape[2])
    feats = lax.all_gather(gathered, "t", axis=0, tiled=True)

    mixed = attend(queries, feats, kv_weight)
    mixed = lax.all_gather(mixed, "t", axis=0, tiled=False)
    return project(mixed, w_cols)


def solution(mesh):
    fine = Mesh(mesh.devices.reshape(NY, NZ, NX, NC, NT), DP + ("t",))
    return jax.shard_map(
        shards,
        mesh=fine,
        in_specs=(
            P(DP, "t"),
            P(DP, "t"),
            P(None, None, "t"),
            P("t", DP),
            P(DP, None),
        ),
        out_specs=P(DP, "t"),
        check_vma=False,
    )
```

```python
import math

import jax
import jax.numpy as jnp
from jax import lax
from jax.experimental import pallas as pl
from jax.experimental.pallas import tpu as pltpu
from jax.sharding import Mesh
from jax.sharding import PartitionSpec as P

HEAD = 128
SPAN = 64
ROWBLK = 16
LANES = 128
NY, NZ, NX, NC, NT = 4, 4, 4, 2, 4
DP = ("y", "z", "x", "c")
PEERS = ("y", "x", "c")
LAST_DIMS = (((1,), (1,)), ((), ()))
IN_SMEM = pl.BlockSpec(memory_space=pltpu.SMEM)
IN_VMEM = pl.BlockSpec(memory_space=pltpu.VMEM)
IN_HBM = pl.BlockSpec(memory_space=pltpu.HBM)
ANYWHERE = pl.BlockSpec(memory_space=pl.ANY)
PARAMS = pltpu.CompilerParams(vmem_limit_bytes=24 * 2**20)


def like(value):
    return jax.ShapeDtypeStruct(value.shape, value.dtype)


def slot_of(shard):
    per_y = NZ * NX * NC
    peer = shard // per_y * (NX * NC) + shard % (NX * NC)
    return peer * NZ + shard // (NX * NC) % NZ


def want(nbr_map, enc_blocks):
    z = jnp.arange(LANES, dtype=jnp.int32)[None, :]
    peer = jnp.arange(NY * NX * NC, dtype=jnp.int32)[:, None]
    shard = (peer // (NX * NC) * NZ + z) * (NX * NC) + peer % (NX * NC)
    shard = jnp.where(z < NZ, shard, NY * NZ * NX * NC)
    row_block = nbr_map[:, :, None, None] - shard * enc_blocks
    wanted = jnp.where((row_block >= 0) & (row_block < enc_blocks), row_block, 0)
    return jnp.sum(wanted, axis=(0, 1))[:, None, :]


def attend_kernel(q_ref, feat_ref, kv_ref, mixed_ref):
    spans = q_ref.shape[0] // SPAN
    per_span = feat_ref.shape[1] // spans
    heads = q_ref.shape[1] // HEAD
    feats = feat_ref[...].T
    keys = jnp.dot(feats, kv_ref[0], preferred_element_type=jnp.float32)
    keys = keys.astype(jnp.bfloat16)
    values = jnp.dot(feats, kv_ref[1], preferred_element_type=jnp.float32)
    values = values.astype(jnp.bfloat16)
    for span in range(spans):
        for head in range(heads):
            tokens = slice(span * SPAN, (span + 1) * SPAN)
            rows = slice(span * per_span, (span + 1) * per_span)
            lanes = slice(head * HEAD, (head + 1) * HEAD)
            scores = lax.dot_general(
                q_ref[tokens, lanes], keys[rows, lanes], LAST_DIMS,
                preferred_element_type=jnp.float32,
            ) * (1.0 / math.sqrt(HEAD))
            exponent = jnp.exp(scores - jnp.max(scores, axis=-1, keepdims=True))
            weights = exponent / jnp.sum(exponent, axis=-1, keepdims=True)
            mixed = jnp.dot(
                weights.astype(jnp.bfloat16), values[rows, lanes],
                preferred_element_type=jnp.float32,
            )
            mixed_ref[tokens, lanes] = mixed.astype(jnp.bfloat16)


def attend(queries, feats, kv_weight):
    return pl.pallas_call(
        attend_kernel,
        in_specs=[IN_VMEM, IN_VMEM, IN_VMEM],
        out_shape=like(queries),
        compiler_params=PARAMS,
        name="attend",
    )(queries, feats, kv_weight)


def pick_kernel(z_ref, served_ref, *refs):
    held_refs, (chosen_ref, rows_ref) = refs[:NZ], refs[NZ:]
    features, rows = chosen_ref.shape[-1], held_refs[0].shape[1]
    for bits, held_ref in enumerate(held_refs):
        rows_ref[bits * rows : (bits + 1) * rows] = held_ref[:features].T
    base = [(z_ref[0] ^ z) * rows for z in range(NZ)]
    for peer in range(chosen_ref.shape[0]):
        for z in range(NZ):
            start = pl.multiple_of(base[z] + served_ref[peer, 0, z] * ROWBLK, ROWBLK)
            chosen_ref[peer, z] = rows_ref[pl.ds(start, ROWBLK)]


def pick(my_z, served, held):
    features, rows = held[0].shape
    chosen = (served.shape[0], NZ, ROWBLK, features)
    return pl.pallas_call(
        pick_kernel,
        in_specs=[IN_SMEM, IN_SMEM] + [IN_VMEM] * NZ,
        out_shape=jax.ShapeDtypeStruct(chosen, held[0].dtype),
        scratch_shapes=[pltpu.VMEM((NZ * rows, features), held[0].dtype)],
        compiler_params=PARAMS,
        name="pick",
    )(my_z, served, *held)


def take_kernel(slot_ref, arrived_ref, feats_ref, rows_ref):
    spans, per_span = slot_ref.shape
    for span in range(spans):
        for at in range(per_span):
            to = (span * per_span + at) * ROWBLK
            rows_ref[to : to + ROWBLK] = arrived_ref[slot_ref[span, at]]
    feats_ref[...] = rows_ref[...].T


def take(slots, arrived):
    rows, features = slots.size * ROWBLK, arrived.shape[2]
    return pl.pallas_call(
        take_kernel,
        in_specs=[IN_SMEM, IN_VMEM],
        out_shape=jax.ShapeDtypeStruct((features, rows), arrived.dtype),
        scratch_shapes=[pltpu.VMEM((rows, features), arrived.dtype)],
        compiler_params=PARAMS,
        name="take",
    )(slots, arrived)


def project_kernel(mixed_ref, far_ref, out_ref, w_ref, total_ref, sems):
    groups, cols, _ = w_ref.shape
    copies = [
        pltpu.make_async_copy(far_ref.at[group], w_ref.at[group], sems.at[group])
        for group in range(groups)
    ]
    for copy in copies:
        copy.start()
    step = 256
    for group in range(groups):
        copies[group].wait()
        for col in range(0, cols, step):
            here = slice(col, col + step)
            partial = lax.dot_general(
                mixed_ref[group], w_ref[group, here], LAST_DIMS,
                preferred_element_type=jnp.float32,
            )
            partial = partial.astype(jnp.bfloat16).astype(jnp.float32)
            total = partial if group == 0 else total_ref[:, here] + partial
            if group == groups - 1:
                out_ref[:, here] = total.astype(jnp.bfloat16)
            else:
                total_ref[:, here] = total


def project(mixed, w_cols):
    groups, cols, _ = w_cols.shape
    tokens = mixed.shape[1]
    return pl.pallas_call(
        project_kernel,
        in_specs=[IN_VMEM, IN_HBM],
        out_shape=jax.ShapeDtypeStruct((tokens, cols), jnp.bfloat16),
        scratch_shapes=[
            pltpu.VMEM(w_cols.shape, w_cols.dtype),
            pltpu.VMEM((tokens, cols), jnp.float32),
            pltpu.SemaphoreType.DMA((groups,)),
        ],
        compiler_params=PARAMS,
        name="project",
    )(mixed, pltpu.with_memory_space_constraint(w_cols, pltpu.HBM))


def device_index(y, z, x, c, t):
    return (((y * NZ + z) * NX + x) * NC + c) * NT + t


def to_column_owner():
    pairs = []
    for y in range(NY):
        for block in range(NZ * NX * NC):
            z, x, c = block // (NX * NC), block // NC % NX, block % NC
            new_x, new_z, new_c = block // (NZ * NC), block // NC % NZ, block % NC
            for t in range(NT):
                target = device_index(t, new_z, new_x, new_c, y)
                pairs.append((device_index(y, z, x, c, t), target))
    return pairs


def from_z(value, bits):
    return lax.ppermute(value, "z", [(z, z ^ bits) for z in range(NZ)])


def shards(queries, encodings, kv_weight, w_out, nbr_map):
    enc_blocks = encodings.shape[0] // ROWBLK
    features = encodings.shape[1]
    my_z = lax.axis_index("z").astype(jnp.int32).reshape(1)
    wanted = want(nbr_map, enc_blocks)
    piece, wanted = lax.optimization_barrier((w_out.T, wanted))
    piece = lax.ppermute(piece, DP + ("t",), to_column_owner())

    feats = encodings.T
    served = lax.all_to_all(wanted, PEERS, split_axis=0, concat_axis=0, tiled=True)
    one, two = from_z(feats, 1), from_z(feats, 2)
    two, served, piece = lax.optimization_barrier((two, served, piece))
    chosen = pick(my_z, served, [feats, one, two, from_z(two, 1)])
    arrived = lax.all_to_all(chosen, PEERS, split_axis=0, concat_axis=0, tiled=True)

    chosen, piece = lax.optimization_barrier((chosen, piece))
    four = lax.all_gather(piece, ("z", "c"), axis=0, tiled=True)
    pieces = jnp.broadcast_to(four[None], (NY * NX,) + four.shape)

    slots = slot_of(nbr_map // enc_blocks)
    slots, pieces = lax.optimization_barrier((slots, pieces))
    gathered = take(slots, arrived.reshape(-1, ROWBLK, features))
    gathered, pieces = lax.optimization_barrier((gathered, pieces))
    w_cols = lax.all_to_all(pieces, ("y", "x"), split_axis=0, concat_axis=0, tiled=True)
    w_cols = w_cols.reshape(NY, -1, w_cols.shape[2])
    feats = lax.all_gather(gathered, "t", axis=0, tiled=True)

    mixed = attend(queries, feats, kv_weight)
    mixed = lax.all_gather(mixed, "t", axis=0, tiled=False)
    return project(mixed, w_cols)


def solution(mesh):
    fine = Mesh(mesh.devices.reshape(NY, NZ, NX, NC, NT), DP + ("t",))
    return jax.shard_map(
        shards,
        mesh=fine,
        in_specs=(
            P(DP, "t"),
            P(DP, "t"),
            P(None, None, "t"),
            P("t", DP),
            P(DP, None),
        ),
        out_specs=P(DP, "t"),
        check_vma=False,
    )
```

```python
import math

import jax
import jax.numpy as jnp
from jax import lax
from jax.experimental import pallas as pl
from jax.experimental.pallas import tpu as pltpu
from jax.sharding import Mesh
from jax.sharding import PartitionSpec as P

HEAD = 128
SPAN = 64
ROWBLK = 16
LANES = 128
NY, NZ, NX, NC, NT = 4, 4, 4, 2, 4
DP = ("y", "z", "x", "c")
PEERS = ("y", "x", "c")
LAST_DIMS = (((1,), (1,)), ((), ()))
IN_SMEM = pl.BlockSpec(memory_space=pltpu.SMEM)
IN_VMEM = pl.BlockSpec(memory_space=pltpu.VMEM)
IN_HBM = pl.BlockSpec(memory_space=pltpu.HBM)
ANYWHERE = pl.BlockSpec(memory_space=pl.ANY)
PARAMS = pltpu.CompilerParams(vmem_limit_bytes=24 * 2**20)


def like(value):
    return jax.ShapeDtypeStruct(value.shape, value.dtype)


def slot_of(shard):
    per_y = NZ * NX * NC
    peer = shard // per_y * (NX * NC) + shard % (NX * NC)
    return peer * NZ + shard // (NX * NC) % NZ


def want(nbr_map, enc_blocks):
    z = jnp.arange(LANES, dtype=jnp.int32)[None, :]
    peer = jnp.arange(NY * NX * NC, dtype=jnp.int32)[:, None]
    shard = (peer // (NX * NC) * NZ + z) * (NX * NC) + peer % (NX * NC)
    shard = jnp.where(z < NZ, shard, NY * NZ * NX * NC)
    row_block = nbr_map[:, :, None, None] - shard * enc_blocks
    wanted = jnp.where((row_block >= 0) & (row_block < enc_blocks), row_block, 0)
    return jnp.sum(wanted, axis=(0, 1))[:, None, :]


def attend_kernel(q_ref, feat_ref, kv_ref, mixed_ref):
    spans = q_ref.shape[0] // SPAN
    per_span = feat_ref.shape[1] // spans
    heads = q_ref.shape[1] // HEAD
    feats = feat_ref[...].T
    keys = jnp.dot(feats, kv_ref[0], preferred_element_type=jnp.float32)
    keys = keys.astype(jnp.bfloat16)
    values = jnp.dot(feats, kv_ref[1], preferred_element_type=jnp.float32)
    values = values.astype(jnp.bfloat16)
    scale = 1.0 / math.sqrt(HEAD)
    units = []
    for span in range(spans):
        for head in range(heads):
            tokens = slice(span * SPAN, (span + 1) * SPAN)
            rows = slice(span * per_span, (span + 1) * per_span)
            units.append((tokens, rows, slice(head * HEAD, (head + 1) * HEAD)))
    scores = [
        lax.dot_general(
            q_ref[tokens, lanes], keys[rows, lanes], LAST_DIMS,
            preferred_element_type=jnp.float32,
        ) * scale
        for tokens, rows, lanes in units
    ]
    weights = []
    for score in scores:
        exponent = jnp.exp(score - jnp.max(score, axis=-1, keepdims=True))
        weight = exponent / jnp.sum(exponent, axis=-1, keepdims=True)
        weights.append(weight.astype(jnp.bfloat16))
    for weight, (tokens, rows, lanes) in zip(weights, units):
        mixed = jnp.dot(weight, values[rows, lanes], preferred_element_type=jnp.float32)
        mixed_ref[tokens, lanes] = mixed.astype(jnp.bfloat16)


def attend(queries, feats, kv_weight):
    return pl.pallas_call(
        attend_kernel,
        in_specs=[IN_VMEM, IN_VMEM, IN_VMEM],
        out_shape=like(queries),
        compiler_params=PARAMS,
        name="attend",
    )(queries, feats, kv_weight)


def pick_kernel(z_ref, served_ref, *refs):
    held_refs, (chosen_ref, rows_ref) = refs[:NZ], refs[NZ:]
    features, rows = chosen_ref.shape[-1], held_refs[0].shape[1]
    for bits, held_ref in enumerate(held_refs):
        rows_ref[bits * rows : (bits + 1) * rows] = held_ref[:features].T
    base = [(z_ref[0] ^ z) * rows for z in range(NZ)]
    for peer in range(chosen_ref.shape[0]):
        for z in range(NZ):
            start = pl.multiple_of(base[z] + served_ref[peer, 0, z] * ROWBLK, ROWBLK)
            chosen_ref[peer, z] = rows_ref[pl.ds(start, ROWBLK)]


def pick(my_z, served, held):
    features, rows = held[0].shape
    chosen = (served.shape[0], NZ, ROWBLK, features)
    return pl.pallas_call(
        pick_kernel,
        in_specs=[IN_SMEM, IN_SMEM] + [IN_VMEM] * NZ,
        out_shape=jax.ShapeDtypeStruct(chosen, held[0].dtype),
        scratch_shapes=[pltpu.VMEM((NZ * rows, features), held[0].dtype)],
        compiler_params=PARAMS,
        name="pick",
    )(my_z, served, *held)


def take_kernel(slot_ref, arrived_ref, feats_ref, rows_ref):
    spans, per_span = slot_ref.shape
    for span in range(spans):
        for at in range(per_span):
            to = (span * per_span + at) * ROWBLK
            rows_ref[to : to + ROWBLK] = arrived_ref[slot_ref[span, at]]
    feats_ref[...] = rows_ref[...].T


def take(slots, arrived):
    rows, features = slots.size * ROWBLK, arrived.shape[2]
    return pl.pallas_call(
        take_kernel,
        in_specs=[IN_SMEM, IN_VMEM],
        out_shape=jax.ShapeDtypeStruct((features, rows), arrived.dtype),
        scratch_shapes=[pltpu.VMEM((rows, features), arrived.dtype)],
        compiler_params=PARAMS,
        name="take",
    )(slots, arrived)


def project_kernel(mixed_ref, far_ref, out_ref, w_ref, total_ref, sems):
    groups, cols, _ = w_ref.shape
    copies = [
        pltpu.make_async_copy(far_ref.at[group], w_ref.at[group], sems.at[group])
        for group in range(groups)
    ]
    for copy in copies:
        copy.start()
    step = 256
    for group in range(groups):
        copies[group].wait()
        for col in range(0, cols, step):
            here = slice(col, col + step)
            partial = lax.dot_general(
                mixed_ref[group], w_ref[group, here], LAST_DIMS,
                preferred_element_type=jnp.float32,
            )
            partial = partial.astype(jnp.bfloat16).astype(jnp.float32)
            total = partial if group == 0 else total_ref[:, here] + partial
            if group == groups - 1:
                out_ref[:, here] = total.astype(jnp.bfloat16)
            else:
                total_ref[:, here] = total


def project(mixed, w_cols):
    groups, cols, _ = w_cols.shape
    tokens = mixed.shape[1]
    return pl.pallas_call(
        project_kernel,
        in_specs=[IN_VMEM, IN_HBM],
        out_shape=jax.ShapeDtypeStruct((tokens, cols), jnp.bfloat16),
        scratch_shapes=[
            pltpu.VMEM(w_cols.shape, w_cols.dtype),
            pltpu.VMEM((tokens, cols), jnp.float32),
            pltpu.SemaphoreType.DMA((groups,)),
        ],
        compiler_params=PARAMS,
        name="project",
    )(mixed, pltpu.with_memory_space_constraint(w_cols, pltpu.HBM))


def device_index(y, z, x, c, t):
    return (((y * NZ + z) * NX + x) * NC + c) * NT + t


def to_column_owner():
    pairs = []
    for y in range(NY):
        for block in range(NZ * NX * NC):
            z, x, c = block // (NX * NC), block // NC % NX, block % NC
            new_x, new_z, new_c = block // (NZ * NC), block // NC % NZ, block % NC
            for t in range(NT):
                target = device_index(t, new_z, new_x, new_c, y)
                pairs.append((device_index(y, z, x, c, t), target))
    return pairs


def from_z(value, bits):
    return lax.ppermute(value, "z", [(z, z ^ bits) for z in range(NZ)])


def shards(queries, encodings, kv_weight, w_out, nbr_map):
    enc_blocks = encodings.shape[0] // ROWBLK
    features = encodings.shape[1]
    my_z = lax.axis_index("z").astype(jnp.int32).reshape(1)
    wanted = want(nbr_map, enc_blocks)
    piece, wanted = lax.optimization_barrier((w_out.T, wanted))
    piece = lax.ppermute(piece, DP + ("t",), to_column_owner())

    feats = encodings.T
    served = lax.all_to_all(wanted, PEERS, split_axis=0, concat_axis=0, tiled=True)
    one, two = from_z(feats, 1), from_z(feats, 2)
    two, served, piece = lax.optimization_barrier((two, served, piece))
    slots = slot_of(nbr_map // enc_blocks)
    one, slots = lax.optimization_barrier((one, slots))
    chosen = pick(my_z, served, [feats, one, two, from_z(two, 1)])
    arrived = lax.all_to_all(chosen, PEERS, split_axis=0, concat_axis=0, tiled=True)

    chosen, piece = lax.optimization_barrier((chosen, piece))
    four = lax.all_gather(piece, ("z", "c"), axis=0, tiled=True)
    pieces = jnp.broadcast_to(four[None], (NY * NX,) + four.shape)

    slots, pieces = lax.optimization_barrier((slots, pieces))
    gathered = take(slots, arrived.reshape(-1, ROWBLK, features))
    gathered, pieces = lax.optimization_barrier((gathered, pieces))
    w_cols = lax.all_to_all(pieces, ("y", "x"), split_axis=0, concat_axis=0, tiled=True)
    w_cols = w_cols.reshape(NY, -1, w_cols.shape[2])
    feats = lax.all_gather(gathered, "t", axis=0, tiled=True)

    mixed = attend(queries, feats, kv_weight)
    mixed = lax.all_gather(mixed, "t", axis=0, tiled=False)
    return project(mixed, w_cols)


def solution(mesh):
    fine = Mesh(mesh.devices.reshape(NY, NZ, NX, NC, NT), DP + ("t",))
    return jax.shard_map(
        shards,
        mesh=fine,
        in_specs=(
            P(DP, "t"),
            P(DP, "t"),
            P(None, None, "t"),
            P("t", DP),
            P(DP, None),
        ),
        out_specs=P(DP, "t"),
        check_vma=False,
    )
```

```python
import math

import jax
import jax.numpy as jnp
from jax import lax
from jax.experimental import pallas as pl
from jax.experimental.pallas import tpu as pltpu
from jax.sharding import Mesh
from jax.sharding import PartitionSpec as P

HEAD = 128
SPAN = 64
ROWBLK = 16
LANES = 128
NY, NZ, NX, NC, NT = 4, 4, 4, 2, 4
DP = ("y", "z", "x", "c")
PEERS = ("y", "x", "c")
LAST_DIMS = (((1,), (1,)), ((), ()))
IN_SMEM = pl.BlockSpec(memory_space=pltpu.SMEM)
IN_VMEM = pl.BlockSpec(memory_space=pltpu.VMEM)
IN_HBM = pl.BlockSpec(memory_space=pltpu.HBM)
ANYWHERE = pl.BlockSpec(memory_space=pl.ANY)
PARAMS = pltpu.CompilerParams(vmem_limit_bytes=24 * 2**20)


def like(value):
    return jax.ShapeDtypeStruct(value.shape, value.dtype)


def slot_of(shard):
    per_y = NZ * NX * NC
    peer = shard // per_y * (NX * NC) + shard % (NX * NC)
    return peer * NZ + shard // (NX * NC) % NZ


def want(nbr_map, enc_blocks):
    z = jnp.arange(LANES, dtype=jnp.int32)[None, :]
    peer = jnp.arange(NY * NX * NC, dtype=jnp.int32)[:, None]
    shard = (peer // (NX * NC) * NZ + z) * (NX * NC) + peer % (NX * NC)
    shard = jnp.where(z < NZ, shard, NY * NZ * NX * NC)
    row_block = nbr_map[:, :, None, None] - shard * enc_blocks
    wanted = jnp.where((row_block >= 0) & (row_block < enc_blocks), row_block, 0)
    return jnp.sum(wanted, axis=(0, 1))[:, None, :]


def attend_kernel(q_ref, feat_ref, kv_ref, mixed_ref):
    spans = q_ref.shape[0] // SPAN
    per_span = feat_ref.shape[1] // spans
    heads = q_ref.shape[1] // HEAD
    feats = feat_ref[...].T
    keys = jnp.dot(feats, kv_ref[0], preferred_element_type=jnp.float32)
    keys = keys.astype(jnp.bfloat16)
    values = jnp.dot(feats, kv_ref[1], preferred_element_type=jnp.float32)
    values = values.astype(jnp.bfloat16)
    scale = 1.0 / math.sqrt(HEAD)
    units = []
    for span in range(spans):
        for head in range(heads):
            tokens = slice(span * SPAN, (span + 1) * SPAN)
            rows = slice(span * per_span, (span + 1) * per_span)
            units.append((tokens, rows, slice(head * HEAD, (head + 1) * HEAD)))
    scores = [
        lax.dot_general(
            q_ref[tokens, lanes], keys[rows, lanes], LAST_DIMS,
            preferred_element_type=jnp.float32,
        ) * scale
        for tokens, rows, lanes in units
    ]
    weights = []
    for score in scores:
        exponent = jnp.exp(score - jnp.max(score, axis=-1, keepdims=True))
        weight = exponent / jnp.sum(exponent, axis=-1, keepdims=True)
        weights.append(weight.astype(jnp.bfloat16))
    for weight, (tokens, rows, lanes) in zip(weights, units):
        mixed = jnp.dot(weight, values[rows, lanes], preferred_element_type=jnp.float32)
        mixed_ref[tokens, lanes] = mixed.astype(jnp.bfloat16)


def attend(queries, feats, kv_weight):
    return pl.pallas_call(
        attend_kernel,
        in_specs=[IN_VMEM, IN_VMEM, IN_VMEM],
        out_shape=like(queries),
        compiler_params=PARAMS,
        name="attend",
    )(queries, feats, kv_weight)


def pick_kernel(z_ref, served_ref, *refs):
    held_refs, (chosen_ref, rows_ref) = refs[:NZ], refs[NZ:]
    features, rows = chosen_ref.shape[-1], held_refs[0].shape[1]
    for bits, held_ref in enumerate(held_refs):
        rows_ref[bits * rows : (bits + 1) * rows] = held_ref[:features].T
    base = [(z_ref[0] ^ z) * rows for z in range(NZ)]
    for peer in range(chosen_ref.shape[0]):
        for z in range(NZ):
            start = pl.multiple_of(base[z] + served_ref[peer, 0, z] * ROWBLK, ROWBLK)
            chosen_ref[peer, z] = rows_ref[pl.ds(start, ROWBLK)]


def pick(my_z, served, held):
    features, rows = held[0].shape
    chosen = (served.shape[0], NZ, ROWBLK, features)
    return pl.pallas_call(
        pick_kernel,
        in_specs=[IN_SMEM, IN_SMEM] + [IN_VMEM] * NZ,
        out_shape=jax.ShapeDtypeStruct(chosen, held[0].dtype),
        scratch_shapes=[pltpu.VMEM((NZ * rows, features), held[0].dtype)],
        compiler_params=PARAMS,
        name="pick",
    )(my_z, served, *held)


def take_kernel(slot_ref, arrived_ref, rows_ref):
    spans, per_span = slot_ref.shape
    for span in range(spans):
        for at in range(per_span):
            to = (span * per_span + at) * ROWBLK
            rows_ref[to : to + ROWBLK] = arrived_ref[slot_ref[span, at]]


def take(slots, arrived):
    return pl.pallas_call(
        take_kernel,
        in_specs=[IN_SMEM, IN_VMEM],
        out_shape=jax.ShapeDtypeStruct(
            (slots.size * ROWBLK, arrived.shape[2]), arrived.dtype
        ),
        compiler_params=PARAMS,
        name="take",
    )(slots, arrived)


def project_kernel(mixed_ref, far_ref, out_ref, w_ref, total_ref, sems):
    groups, cols, _ = w_ref.shape
    copies = [
        pltpu.make_async_copy(far_ref.at[group], w_ref.at[group], sems.at[group])
        for group in range(groups)
    ]
    for copy in copies:
        copy.start()
    step = 256
    for group in range(groups):
        copies[group].wait()
        for col in range(0, cols, step):
            here = slice(col, col + step)
            partial = lax.dot_general(
                mixed_ref[group], w_ref[group, here], LAST_DIMS,
                preferred_element_type=jnp.float32,
            )
            partial = partial.astype(jnp.bfloat16).astype(jnp.float32)
            total = partial if group == 0 else total_ref[:, here] + partial
            if group == groups - 1:
                out_ref[:, here] = total.astype(jnp.bfloat16)
            else:
                total_ref[:, here] = total


def project(mixed, w_cols):
    groups, cols, _ = w_cols.shape
    tokens = mixed.shape[1]
    return pl.pallas_call(
        project_kernel,
        in_specs=[IN_VMEM, IN_HBM],
        out_shape=jax.ShapeDtypeStruct((tokens, cols), jnp.bfloat16),
        scratch_shapes=[
            pltpu.VMEM(w_cols.shape, w_cols.dtype),
            pltpu.VMEM((tokens, cols), jnp.float32),
            pltpu.SemaphoreType.DMA((groups,)),
        ],
        compiler_params=PARAMS,
        name="project",
    )(mixed, pltpu.with_memory_space_constraint(w_cols, pltpu.HBM))


def device_index(y, z, x, c, t):
    return (((y * NZ + z) * NX + x) * NC + c) * NT + t


def to_column_owner():
    pairs = []
    for y in range(NY):
        for block in range(NZ * NX * NC):
            z, x, c = block // (NX * NC), block // NC % NX, block % NC
            new_x, new_z, new_c = block // (NZ * NC), block // NC % NZ, block % NC
            for t in range(NT):
                target = device_index(t, new_z, new_x, new_c, y)
                pairs.append((device_index(y, z, x, c, t), target))
    return pairs


def from_z(value, bits):
    return lax.ppermute(value, "z", [(z, z ^ bits) for z in range(NZ)])


def shards(queries, encodings, kv_weight, w_out, nbr_map):
    enc_blocks = encodings.shape[0] // ROWBLK
    features = encodings.shape[1]
    my_z = lax.axis_index("z").astype(jnp.int32).reshape(1)
    wanted = want(nbr_map, enc_blocks)
    piece, wanted = lax.optimization_barrier((w_out.T, wanted))
    piece = lax.ppermute(piece, DP + ("t",), to_column_owner())

    feats = encodings.T
    served = lax.all_to_all(wanted, PEERS, split_axis=0, concat_axis=0, tiled=True)
    one, two = from_z(feats, 1), from_z(feats, 2)
    two, served, piece = lax.optimization_barrier((two, served, piece))
    slots = slot_of(nbr_map // enc_blocks)
    one, slots = lax.optimization_barrier((one, slots))
    chosen = pick(my_z, served, [feats, one, two, from_z(two, 1)])
    arrived = lax.all_to_all(chosen, PEERS, split_axis=0, concat_axis=0, tiled=True)

    chosen, piece = lax.optimization_barrier((chosen, piece))
    four = lax.all_gather(piece, ("z", "c"), axis=0, tiled=True)
    pieces = jnp.broadcast_to(four[None], (NY * NX,) + four.shape)

    slots, pieces = lax.optimization_barrier((slots, pieces))
    gathered = take(slots, arrived.reshape(-1, ROWBLK, features))
    gathered, pieces = lax.optimization_barrier((gathered, pieces))
    w_cols = lax.all_to_all(pieces, ("y", "x"), split_axis=0, concat_axis=0, tiled=True)
    w_cols = w_cols.reshape(NY, -1, w_cols.shape[2])
    feats = lax.all_gather(gathered.T, "t", axis=0, tiled=True)

    mixed = attend(queries, feats, kv_weight)
    mixed = lax.all_gather(mixed, "t", axis=0, tiled=False)
    return project(mixed, w_cols)


def solution(mesh):
    fine = Mesh(mesh.devices.reshape(NY, NZ, NX, NC, NT), DP + ("t",))
    return jax.shard_map(
        shards,
        mesh=fine,
        in_specs=(
            P(DP, "t"),
            P(DP, "t"),
            P(None, None, "t"),
            P("t", DP),
            P(DP, None),
        ),
        out_specs=P(DP, "t"),
        check_vma=False,
    )
```
